32 devices in a mesh: fsdp: 8 (over y, x, core), ctx: 4 (over z).
Axes of the slice: x: 2, y: 2, z: 4, core: 2. Of those that a mesh axis runs over, the one named last changes fastest.
Arguments:
- tokens: bfloat16 [8, 2048, 1024], P('fsdp', 'ctx'), may hold values from -6 to 6
- query_key_value_weight: bfloat16 [1024, 3072], P('fsdp'), may hold values from -0.1875 to 0.1875
- attention_output_weight: bfloat16 [1024, 1024], P('fsdp'), may hold values from -6 to 6
- geglu_input_weight: bfloat16 [1024, 5248], P('fsdp'), may hold values from -0.1875 to 0.1875
- geglu_output_weight: bfloat16 [2624, 1024], P(None, 'fsdp'), may hold values from -0.125 to 0.125
- gain_one: bfloat16 [1024], P('fsdp'), may hold values from 0.5 to 1.5
- gain_two: bfloat16 [1024], P('fsdp'), may hold values from 0.5 to 1.5
- cotangent: bfloat16 [8, 2048, 1024], P('fsdp', 'ctx'), may hold values from -6 to 6
Outputs:
- mixed: bfloat16 [8, 2048, 1024], P('fsdp', 'ctx')
- grad_tokens: float32 [8, 2048, 1024], P('fsdp', 'ctx')
- grad_qkv: float32 [1024, 3072], P('fsdp')
- grad_attn_out: float32 [1024, 1024], P('fsdp')
- grad_in: float32 [1024, 5248], P('fsdp')
- grad_out: float32 [2624, 1024], P(None, 'fsdp')
- grad_gain_one: float32 [1024], P('fsdp')
- grad_gain_two: float32 [1024], P('fsdp')
The draws below stay inside these ranges and needn't reach their ends.
All inputs are finite; a program needn't handle non-finite values.
Results may differ from the reference program's by a relative error of at most 0.023.
Values may be sent and summed in bfloat16 or wider, within the bound.
A program may use at most 384 MiB of HBM per device.

```python
import jax
import jax.numpy as jnp
from jax import lax

D = 1024
HEADS = 16
HEAD_DIM = 64
FF = 2624
SEQ_LEN = 2048
SEQS = 8


def block_levels(stream_key, extent, pieces, smallest, high):
    def one(dim, parts):
        heights = jax.random.uniform(jax.random.fold_in(jax.random.fold_in(stream_key, 6), dim), (parts,), jnp.float32, smallest / len(pieces), high / len(pieces))
        return jnp.repeat(jnp.exp(heights), extent[dim] // parts).reshape((-1,) + (1,) * (len(extent) - dim - 1))

    level = one(*pieces[0])
    for cut in pieces[1:]:
        level = level * one(*cut)
    return level


def noise(rng, extent, width, reach, split=(), held_as=jnp.bfloat16):
    factor_of = block_levels(rng, extent, split, -0.22, 0.18) if split else 1.0
    values = jax.random.normal(rng, extent, jnp.float32) * width * factor_of
    return jnp.minimum(jnp.maximum(values, -reach), reach).astype(held_as)


def setup_inputs(seed: int = 0) -> dict:
    splits = jax.random.split(jax.random.key(seed), 9)
    return {
        "tokens": noise(splits[0], (SEQS, SEQ_LEN, D), 1.0, 6.0, ((0, 8), (1, 4))),
        "query_key_value_weight": noise(splits[1], (D, 3 * D), D ** -0.5, 0.1875, ((0, 8),)),
        "attention_output_weight": noise(splits[2], (D, D), (max(1, 3 * D // SEQ_LEN)) ** -0.5, 6.0, ((0, 8),)),
        "geglu_input_weight": noise(splits[3], (D, 2 * FF), D ** -0.5, 0.1875, ((0, 8),)),
        "geglu_output_weight": noise(splits[4], (FF, D), FF ** -0.5, 0.125, ((1, 8),)),
        "gain_one": jnp.clip(1.0 + 0.1 * jax.random.normal(splits[5], (D,), jnp.float32), 0.5, 1.5).astype(jnp.bfloat16),
        "gain_two": jnp.clip(1.0 + 0.1 * jax.random.normal(splits[6], (D,), jnp.float32), 0.5, 1.5).astype(jnp.bfloat16),
        "cotangent": noise(splits[7], (SEQS, SEQ_LEN, D), 1.0, 6.0, ((0, 8), (1, 4))),
    }


EPSILON = 1e-05
ROPE_BASE = 160000.0

@jax.custom_vjp
def low(v):
    return lax.optimization_barrier(v.astype(jnp.bfloat16)).astype(jnp.float32)

@jax.custom_vjp
def low_back(v):
    return v

def low_keep(v):
    return (low(v), None)

def low_pass(kept, grad):
    return (grad,)

def back_keep(v):
    return (v, None)

def back_low(kept, grad):
    return (low(grad),)
low.defvjp(low_keep, low_pass)
low_back.defvjp(back_keep, back_low)

def layer_norm(values, gain):
    row_mean = lax.optimization_barrier(jnp.mean(values, -1, keepdims=True))
    centered = values - row_mean
    variance = lax.optimization_barrier(jnp.mean(centered * centered, -1, keepdims=True))
    return centered * lax.rsqrt(variance + EPSILON) * gain

def rope_tables():
    positions = jnp.arange(SEQ_LEN, dtype=jnp.float32)
    inv_freq = ROPE_BASE ** (-(jnp.arange(HEAD_DIM // 2, dtype=jnp.float32) * 2.0 / HEAD_DIM))
    angles = positions[:, None] * inv_freq[None, :]
    angles = jnp.concatenate([angles, angles], -1)
    return (jnp.cos(angles)[:, None, :], jnp.sin(angles)[:, None, :])

def rotate(vectors, cosine, sine):
    half_dim = vectors.shape[-1] // 2
    turned = jnp.concatenate([-vectors[..., half_dim:], vectors[..., :half_dim]], -1)
    return vectors * cosine + turned * sine

def attend(triple):
    query, keys, values = triple
    scores = jnp.einsum('qhd,khd->hqk', query, keys, precision=lax.Precision.HIGHEST) * HEAD_DIM ** (-0.5)
    scores = low_back(scores)
    peak = lax.optimization_barrier(jnp.max(scores, -1, keepdims=True))
    expd = jnp.exp(scores - peak)
    probs = low(expd / lax.optimization_barrier(jnp.sum(expd, -1, keepdims=True)))
    result = jnp.einsum('hqk,khd->qhd', probs, values, precision=lax.Precision.HIGHEST)
    return result.reshape(SEQ_LEN, D)

def forward(tokens, query_key_value_weight, attention_output_weight, geglu_input_weight, geglu_output_weight, gain_one, gain_two):
    highest_precision = lax.Precision.HIGHEST
    hidden_after_attention = low(layer_norm(tokens, gain_one))
    query_key_value = low_back(jnp.einsum('zmp,pb->zmb', hidden_after_attention, query_key_value_weight, precision=highest_precision))
    cosine, sine = rope_tables()
    shape_heads = (SEQS, SEQ_LEN, HEADS, HEAD_DIM)
    query = low(rotate(query_key_value[..., :D].reshape(shape_heads), cosine, sine))
    keys = low(rotate(query_key_value[..., D:2 * D].reshape(shape_heads), cosine, sine))
    values = low(query_key_value[..., 2 * D:].reshape(shape_heads))
    attended = lax.map(jax.checkpoint(attend), (query, keys, values))
    attention_output = low(low_back(attended))
    middle_activation = tokens + low_back(jnp.einsum('zmp,pb->zmb', attention_output, attention_output_weight, precision=highest_precision))
    hidden_after_feedforward = low(layer_norm(middle_activation, gain_two))
    projected_up_rows = low_back(jnp.einsum('que,eb->qub', hidden_after_feedforward, geglu_input_weight, precision=highest_precision))
    gate_in = projected_up_rows[..., :FF]
    gate_up = projected_up_rows[..., FF:]
    hidden_state = low(jax.nn.gelu(gate_in, approximate=False) * gate_up)
    return middle_activation + jnp.einsum('boc,cy->boy', hidden_state, geglu_output_weight, precision=highest_precision)

def reference(tokens, query_key_value_weight, attention_output_weight, geglu_input_weight, geglu_output_weight, gain_one, gain_two, cotangent):
    floats = [item.astype(jnp.float32) for item in (tokens, query_key_value_weight, attention_output_weight, geglu_input_weight, geglu_output_weight, gain_one, gain_two)]
    output, pullback = jax.vjp(forward, *floats)
    grads = pullback(cotangent.astype(jnp.float32))
    return (output.astype(jnp.bfloat16), grads[0], grads[1], grads[2], grads[3], grads[4], grads[5], grads[6])
```

```python
import math

import jax
import jax.numpy as jnp
from jax import lax
from jax.experimental import pallas as pl
from jax.experimental.pallas import tpu as pltpu
from jax.sharding import PartitionSpec as P

HEADS = 16
HEAD_DIM = 64


EPSILON = 1e-05
ROPE_BASE = 160000.0


def normalize(values):
    row_mean = jnp.mean(values, -1, keepdims=True)
    centered = values - row_mean
    variance = jnp.mean(centered * centered, -1, keepdims=True)
    inv_std = lax.rsqrt(variance + EPSILON)
    return (centered * inv_std, inv_std)


def norm_back(grad_normed, normed, inv_std):
    first_mean = jnp.mean(grad_normed, -1, keepdims=True)
    second_mean = jnp.mean(grad_normed * normed, -1, keepdims=True)
    return inv_std * (grad_normed - first_mean - normed * second_mean)


def rope_tables(first_row, local_rows):
    positions = (first_row + jnp.arange(local_rows, dtype=jnp.int32)).astype(jnp.float32)
    inv_freq = ROPE_BASE ** (-(jnp.arange(HEAD_DIM // 2, dtype=jnp.float32) * 2.0 / HEAD_DIM))
    angles = positions[:, None] * inv_freq[None, :]
    angles = jnp.concatenate([angles, angles], -1)
    return (jnp.cos(angles)[:, None, :], jnp.sin(angles)[:, None, :])


def rotate(vectors, cosine, sine):
    half_dim = vectors.shape[-1] // 2
    turned = jnp.concatenate([-vectors[..., half_dim:], vectors[..., :half_dim]], -1)
    return vectors * cosine + turned * sine


def dot_rows(left, right):
    return lax.dot_general(
        left, right, (((1,), (1,)), ((), ())), preferred_element_type=jnp.float32
    )


def only_head(block, head):
    if block.shape[1] == HEAD_DIM:
        return block
    lane = lax.broadcasted_iota(jnp.int32, block.shape, 1)
    inside = (lane >= head * HEAD_DIM) & (lane < (head + 1) * HEAD_DIM)
    return jnp.where(inside, block.astype(jnp.float32), 0.0).astype(jnp.bfloat16)


def attend_kernel(q_ref, k_ref, v_ref, o_ref, lse_ref, vt_ref):
    @pl.when(pl.program_id(1) == 0)
    def _():
        vt_ref[...] = v_ref[...].T

    results = []
    for head in range(q_ref.shape[1] // HEAD_DIM):
        rows = slice(head * HEAD_DIM, (head + 1) * HEAD_DIM)
        scores = dot_rows(k_ref[...], only_head(q_ref[...], head))
        peak = jnp.max(scores, 0, keepdims=True)
        weights = jnp.exp(scores - peak)
        total = jnp.sum(weights, 0, keepdims=True)
        summed = jnp.dot(
            vt_ref[rows, :], weights.astype(jnp.bfloat16), preferred_element_type=jnp.float32
        )
        results.append(summed / total)
        lse_ref[0, head : head + 1, :] = peak + jnp.log(total)
    o_ref[...] = jnp.concatenate(results, 0).T


def attend_back_kernel(
    q_ref, k_ref, v_ref, o_ref, lse_ref, g_ref, dq_ref, dk_ref, dv_ref, kt_ref, dk_sum, dv_sum
):
    @pl.when(pl.program_id(1) == 0)
    def _():
        kt_ref[...] = k_ref[...].T
        dk_sum[...] = jnp.zeros_like(dk_sum)
        dv_sum[...] = jnp.zeros_like(dv_sum)

    products = (g_ref[...].astype(jnp.float32) * o_ref[...]).T
    results = []
    for head in range(q_ref.shape[1] // HEAD_DIM):
        rows = slice(head * HEAD_DIM, (head + 1) * HEAD_DIM)
        query = only_head(q_ref[...], head)
        grad = only_head(g_ref[...], head)
        probs = jnp.exp(dot_rows(k_ref[...], query) - lse_ref[0, head : head + 1, :])
        delta = jnp.sum(products[rows, :], 0, keepdims=True)
        grad_probs = dot_rows(v_ref[...], grad)
        grad_scores = (probs * (grad_probs - delta)).astype(jnp.bfloat16)
        dv_sum[...] += jnp.dot(
            probs.astype(jnp.bfloat16), grad, preferred_element_type=jnp.float32
        )
        dk_sum[...] += jnp.dot(grad_scores, query, preferred_element_type=jnp.float32)
        results.append(jnp.dot(kt_ref[rows, :], grad_scores, preferred_element_type=jnp.float32))
    dq_ref[...] = (jnp.concatenate(results, 0) * HEAD_DIM**-0.5).T.astype(jnp.bfloat16)

    @pl.when(pl.program_id(1) == pl.num_programs(1) - 1)
    def _():
        dk_ref[...] = dk_sum[...].astype(jnp.bfloat16)
        dv_ref[...] = dv_sum[...].astype(jnp.bfloat16)


def kernel_plan(packed):
    total_rows, width = packed.shape[0], packed.shape[1] // 3
    block_width = 2 * HEAD_DIM if width % (2 * HEAD_DIM) == 0 else width
    groups = width // block_width
    block_rows = min(256, total_rows)
    by_rows = pl.BlockSpec((block_rows, block_width), lambda g, r: (r, g))
    hop = groups if block_width % 128 == 0 else 0
    column = [
        pl.BlockSpec((block_rows, block_width), lambda g, r: (r, g)),
        pl.BlockSpec((total_rows, block_width), lambda g, r: (0, hop + g)),
        pl.BlockSpec((total_rows, block_width), lambda g, r: (0, 2 * hop + g)),
    ]
    heads = block_width // HEAD_DIM
    lse_spec = pl.BlockSpec((1, heads, block_rows), lambda g, r: (g, 0, r))
    lse_shape = jax.ShapeDtypeStruct((groups, heads, total_rows), jnp.float32)
    grid = (groups, total_rows // block_rows)
    params = pltpu.CompilerParams(vmem_limit_bytes=48 * 1024 * 1024)
    return total_rows, width, block_width, by_rows, column, lse_spec, lse_shape, grid, params


def thirds(packed):
    width = packed.shape[1] // 3
    if width % 128 == 0:
        return (packed, packed, packed)
    return tuple(packed[:, part * width : (part + 1) * width] for part in range(3))


def attend(packed):
    total_rows, width, block_width, by_rows, column, lse_spec, lse_shape, grid, params = (
        kernel_plan(packed)
    )
    work = HEAD_DIM * total_rows * total_rows * (width // HEAD_DIM)
    return pl.pallas_call(
        attend_kernel,
        grid=grid,
        in_specs=column,
        out_specs=(by_rows, lse_spec),
        out_shape=(jax.ShapeDtypeStruct((total_rows, width), jnp.float32), lse_shape),
        scratch_shapes=[pltpu.VMEM((block_width, total_rows), jnp.bfloat16)],
        compiler_params=params,
        cost_estimate=pl.CostEstimate(
            flops=8 * work, bytes_accessed=10 * total_rows * width, transcendentals=work // HEAD_DIM
        ),
    )(*thirds(packed))


def attend_back(packed, attended, log_total, grad):
    total_rows, width, block_width, by_rows, column, lse_spec, lse_shape, grid, params = (
        kernel_plan(packed)
    )
    whole = pl.BlockSpec((total_rows, block_width), lambda g, r: (0, g))
    low_shape = jax.ShapeDtypeStruct((total_rows, width), jnp.bfloat16)
    work = HEAD_DIM * total_rows * total_rows * (width // HEAD_DIM)
    return pl.pallas_call(
        attend_back_kernel,
        grid=grid,
        in_specs=column + [by_rows, lse_spec, by_rows],
        out_specs=(by_rows, whole, whole),
        out_shape=(low_shape, low_shape, low_shape),
        scratch_shapes=[
            pltpu.VMEM((block_width, total_rows), jnp.bfloat16),
            pltpu.VMEM((total_rows, block_width), jnp.float32),
            pltpu.VMEM((total_rows, block_width), jnp.float32),
        ],
        compiler_params=params,
        cost_estimate=pl.CostEstimate(
            flops=20 * work, bytes_accessed=20 * total_rows * width, transcendentals=work // HEAD_DIM
        ),
    )(*thirds(packed), attended, log_total, grad)


def to_heads(arrays):
    count, me = lax.axis_size("ctx"), lax.axis_index("ctx")
    width = arrays[0].shape[1] // count
    received = []
    for step in range(count):
        start = lax.rem(me + step, count) * width
        piece = jnp.concatenate(
            [lax.dynamic_slice_in_dim(item, start, width, 1) for item in arrays], 1
        )
        if step:
            piece = lax.ppermute(
                piece, "ctx", [(source, (source + step) % count) for source in range(count)]
            )
        received.append(piece)
    return jnp.concatenate(received, 0)


def to_rows(arrays):
    count, me = lax.axis_size("ctx"), lax.axis_index("ctx")
    rows, width = arrays[0].shape[0] // count, arrays[0].shape[1]
    received = []
    for step in range(count):
        piece = jnp.concatenate([item[step * rows : (step + 1) * rows] for item in arrays], 1)
        if step:
            piece = lax.ppermute(
                piece, "ctx", [(source, (source - step) % count) for source in range(count)]
            )
        received.append(piece)
    start = lax.rem(count - me, count) * width
    results = []
    for number in range(len(arrays)):
        turned = [item[:, number * width : (number + 1) * width] for item in received]
        doubled = jnp.concatenate(turned + turned, 1)
        results.append(lax.dynamic_slice_in_dim(doubled, start, count * width, 1))
    return results


def local(
    tokens,
    query_key_value_weight,
    attention_output_weight,
    geglu_input_weight,
    geglu_output_weight,
    gain_one,
    gain_two,
    cotangent,
):
    local_rows = tokens.shape[1]
    model_width = tokens.shape[2]
    hidden_width = geglu_output_weight.shape[0]
    score_scale = HEAD_DIM ** (-0.5)
    full_qkv, full_attn, full_in, full_out, full_one, full_two = (
        lax.all_gather(query_key_value_weight, "fsdp", axis=0, tiled=True),
        lax.all_gather(attention_output_weight, "fsdp", axis=0, tiled=True),
        lax.all_gather(geglu_input_weight, "fsdp", axis=0, tiled=True),
        lax.all_gather(geglu_output_weight, "fsdp", axis=1, tiled=True),
        *lax.all_gather(jnp.stack([gain_one, gain_two]), "fsdp", axis=1, tiled=True),
    )
    inputs = tokens[0].astype(jnp.float32)
    normed_one, inv_one = normalize(inputs)
    hidden_after_attention = (normed_one * full_one.astype(jnp.float32)).astype(jnp.bfloat16)
    query_key_value = jnp.dot(hidden_after_attention, full_qkv, preferred_element_type=jnp.float32)
    cosine, sine = rope_tables(lax.axis_index("ctx") * local_rows, local_rows)
    head_shape = (local_rows, HEADS, HEAD_DIM)
    query = rotate(query_key_value[:, :model_width].reshape(head_shape), cosine, sine)
    query = (query.astype(jnp.bfloat16) * score_scale).reshape(local_rows, model_width)
    keys = rotate(
        query_key_value[:, model_width : 2 * model_width].reshape(head_shape), cosine, sine
    ).astype(jnp.bfloat16)
    keys = keys.reshape(local_rows, model_width)
    values = query_key_value[:, 2 * model_width :].astype(jnp.bfloat16)
    packed = to_heads((query, keys, values))
    attended, log_total = attend(packed)
    (attn_low,) = to_rows((attended.astype(jnp.bfloat16),))
    middle_activation = inputs + jnp.dot(attn_low, full_attn, preferred_element_type=jnp.float32)
    normed_two, inv_two = normalize(middle_activation)
    hidden_after_feedforward = (normed_two * full_two.astype(jnp.float32)).astype(jnp.bfloat16)
    projected_up_rows = jnp.dot(
        hidden_after_feedforward, full_in, preferred_element_type=jnp.float32
    )
    gate_in = projected_up_rows[:, :hidden_width]
    gate_up = projected_up_rows[:, hidden_width:]
    normal_cdf = 0.5 * (1.0 + lax.erf(gate_in * (1.0 / math.sqrt(2.0))))
    normal_pdf = jnp.exp(-0.5 * gate_in * gate_in) * (1.0 / math.sqrt(2.0 * math.pi))
    activated = gate_in * normal_cdf
    hidden_state = (activated * gate_up).astype(jnp.bfloat16)
    mixed = (
        middle_activation + jnp.dot(hidden_state, full_out, preferred_element_type=jnp.float32)
    ).astype(jnp.bfloat16)
    back_qkv, back_attn, back_in, back_out, back_one, back_two = (
        full_qkv,
        full_attn,
        full_in,
        full_out,
        full_one,
        full_two,
    )
    grad_mixed = cotangent[0]
    grad_wout = jnp.einsum(
        "rf,rd->fd", hidden_state, grad_mixed, preferred_element_type=jnp.float32
    )
    grad_hidden = jnp.einsum("rd,fd->rf", grad_mixed, back_out, preferred_element_type=jnp.float32)
    grad_up = jnp.concatenate(
        [grad_hidden * gate_up * (normal_cdf + gate_in * normal_pdf), grad_hidden * activated], -1
    ).astype(jnp.bfloat16)
    grad_win = jnp.einsum(
        "rd,rf->df", hidden_after_feedforward, grad_up, preferred_element_type=jnp.float32
    )
    grad_htwo = jnp.einsum("rf,df->rd", grad_up, back_in, preferred_element_type=jnp.float32)
    grad_two = jnp.sum(grad_htwo * normed_two, 0)
    grad_middle = grad_mixed.astype(jnp.float32) + norm_back(
        grad_htwo * back_two.astype(jnp.float32), normed_two, inv_two
    )
    part_win = lax.psum_scatter(
        grad_win.astype(jnp.bfloat16), "fsdp", scatter_dimension=0, tiled=True
    )
    part_wout = lax.psum_scatter(
        grad_wout.astype(jnp.bfloat16), "fsdp", scatter_dimension=1, tiled=True
    )
    sum_win, sum_wout = lax.psum((part_win, part_wout), "ctx")
    grad_branch = grad_middle.astype(jnp.bfloat16)
    grad_wattn = jnp.einsum("rd,re->de", attn_low, grad_branch, preferred_element_type=jnp.float32)
    grad_attn = jnp.einsum("re,de->rd", grad_branch, back_attn, preferred_element_type=jnp.float32)
    (grad_heads,) = (to_heads((grad_attn.astype(jnp.bfloat16),)),)
    back_query, back_keys, grad_v = to_rows(attend_back(packed, attended, log_total, grad_heads))
    grad_q = rotate(back_query.reshape(head_shape).astype(jnp.float32), cosine, -sine)
    grad_k = rotate(back_keys.reshape(head_shape).astype(jnp.float32), cosine, -sine)
    grad_qkv_rows = jnp.concatenate(
        [
            grad_q.reshape(local_rows, model_width).astype(jnp.bfloat16),
            grad_k.reshape(local_rows, model_width).astype(jnp.bfloat16),
            grad_v,
        ],
        -1,
    )
    grad_wqkv = jnp.einsum(
        "rd,re->de", hidden_after_attention, grad_qkv_rows, preferred_element_type=jnp.float32
    )
    grad_hone = jnp.einsum("re,de->rd", grad_qkv_rows, back_qkv, preferred_element_type=jnp.float32)
    grad_one = jnp.sum(grad_hone * normed_one, 0)
    grad_inputs = grad_middle + norm_back(
        grad_hone * back_one.astype(jnp.float32), normed_one, inv_one
    )
    part_wqkv = lax.psum_scatter(
        grad_wqkv.astype(jnp.bfloat16), "fsdp", scatter_dimension=0, tiled=True
    )
    part_wattn = lax.psum_scatter(
        grad_wattn.astype(jnp.bfloat16), "fsdp", scatter_dimension=0, tiled=True
    )
    sum_win, sum_wout, part_wqkv, part_wattn = lax.optimization_barrier(
        (sum_win, sum_wout, part_wqkv, part_wattn)
    )
    sum_wqkv, sum_wattn = lax.psum((part_wqkv, part_wattn), "ctx")
    sum_win, sum_wout, sum_wqkv, sum_wattn = (
        item.astype(jnp.float32) for item in (sum_win, sum_wout, sum_wqkv, sum_wattn)
    )
    gains = lax.psum(jnp.stack([grad_one, grad_two]), ("fsdp", "ctx"))
    shard = gain_one.shape[0]
    gains = lax.dynamic_slice_in_dim(gains, lax.axis_index("fsdp") * shard, shard, 1)
    sum_one, sum_two = gains[0], gains[1]
    return (
        mixed[None],
        grad_inputs[None],
        sum_wqkv,
        sum_wattn,
        sum_win,
        sum_wout,
        sum_one,
        sum_two,
    )


def solution(mesh):
    placed = (
        P("fsdp", "ctx", None),
        P("fsdp", None),
        P("fsdp", None),
        P("fsdp", None),
        P(None, "fsdp"),
        P("fsdp"),
        P("fsdp"),
        P("fsdp", "ctx", None),
    )
    return jax.shard_map(
        local,
        mesh=mesh,
        in_specs=placed,
        out_specs=(
            P("fsdp", "ctx", None),
            P("fsdp", "ctx", None),
            P("fsdp", None),
            P("fsdp", None),
            P("fsdp", None),
            P(None, "fsdp"),
            P("fsdp"),
            P("fsdp"),
        ),
        check_vma=False,
    )
```

```python
import math

import jax
import jax.numpy as jnp
from jax import lax
from jax.experimental import pallas as pl
from jax.experimental.pallas import tpu as pltpu
from jax.sharding import PartitionSpec as P

HEADS = 16
HEAD_DIM = 64


EPSILON = 1e-05
ROPE_BASE = 160000.0


def normalize(values):
    row_mean = jnp.mean(values, -1, keepdims=True)
    centered = values - row_mean
    variance = jnp.mean(centered * centered, -1, keepdims=True)
    inv_std = lax.rsqrt(variance + EPSILON)
    return (centered * inv_std, inv_std)


def norm_back(grad_normed, normed, inv_std):
    first_mean = jnp.mean(grad_normed, -1, keepdims=True)
    second_mean = jnp.mean(grad_normed * normed, -1, keepdims=True)
    return inv_std * (grad_normed - first_mean - normed * second_mean)


def rope_tables(first_row, local_rows):
    positions = (first_row + jnp.arange(local_rows, dtype=jnp.int32)).astype(jnp.float32)
    inv_freq = ROPE_BASE ** (-(jnp.arange(HEAD_DIM // 2, dtype=jnp.float32) * 2.0 / HEAD_DIM))
    angles = positions[:, None] * inv_freq[None, :]
    angles = jnp.concatenate([angles, angles], -1)
    return (jnp.cos(angles)[:, None, :], jnp.sin(angles)[:, None, :])


def rotate(vectors, cosine, sine):
    half_dim = vectors.shape[-1] // 2
    turned = jnp.concatenate([-vectors[..., half_dim:], vectors[..., :half_dim]], -1)
    return vectors * cosine + turned * sine


def dot_rows(left, right):
    return lax.dot_general(
        left, right, (((1,), (1,)), ((), ())), preferred_element_type=jnp.float32
    )


def only_head(block, head):
    if block.shape[1] == HEAD_DIM:
        return block
    lane = lax.broadcasted_iota(jnp.int32, block.shape, 1)
    inside = (lane >= head * HEAD_DIM) & (lane < (head + 1) * HEAD_DIM)
    return jnp.where(inside, block.astype(jnp.float32), 0.0).astype(jnp.bfloat16)


def attend_kernel(q_ref, k_ref, v_ref, o_ref, lse_ref, vt_ref):
    @pl.when(pl.program_id(1) == 0)
    def _():
        vt_ref[...] = v_ref[...].T

    results = []
    for head in range(q_ref.shape[1] // HEAD_DIM):
        rows = slice(head * HEAD_DIM, (head + 1) * HEAD_DIM)
        scores = dot_rows(k_ref[...], only_head(q_ref[...], head))
        peak = jnp.max(scores, 0, keepdims=True)
        weights = jnp.exp(scores - peak)
        total = jnp.sum(weights, 0, keepdims=True)
        summed = jnp.dot(
            vt_ref[rows, :], weights.astype(jnp.bfloat16), preferred_element_type=jnp.float32
        )
        results.append(summed / total)
        lse_ref[0, head : head + 1, :] = peak + jnp.log(total)
    o_ref[...] = jnp.concatenate(results, 0).T


def attend_back_kernel(
    q_ref, k_ref, v_ref, o_ref, lse_ref, g_ref, dq_ref, dk_ref, dv_ref, kt_ref, dk_sum, dv_sum
):
    @pl.when(pl.program_id(1) == 0)
    def _():
        kt_ref[...] = k_ref[...].T
        dk_sum[...] = jnp.zeros_like(dk_sum)
        dv_sum[...] = jnp.zeros_like(dv_sum)

    products = (g_ref[...].astype(jnp.float32) * o_ref[...]).T
    results = []
    for head in range(q_ref.shape[1] // HEAD_DIM):
        rows = slice(head * HEAD_DIM, (head + 1) * HEAD_DIM)
        query = only_head(q_ref[...], head)
        grad = only_head(g_ref[...], head)
        probs = jnp.exp(dot_rows(k_ref[...], query) - lse_ref[0, head : head + 1, :])
        delta = jnp.sum(products[rows, :], 0, keepdims=True)
        grad_probs = dot_rows(v_ref[...], grad)
        grad_scores = (probs * (grad_probs - delta)).astype(jnp.bfloat16)
        dv_sum[...] += jnp.dot(
            probs.astype(jnp.bfloat16), grad, preferred_element_type=jnp.float32
        )
        dk_sum[...] += jnp.dot(grad_scores, query, preferred_element_type=jnp.float32)
        results.append(jnp.dot(kt_ref[rows, :], grad_scores, preferred_element_type=jnp.float32))
    dq_ref[...] = (jnp.concatenate(results, 0) * HEAD_DIM**-0.5).T.astype(jnp.bfloat16)

    @pl.when(pl.program_id(1) == pl.num_programs(1) - 1)
    def _():
        dk_ref[...] = dk_sum[...].astype(jnp.bfloat16)
        dv_ref[...] = dv_sum[...].astype(jnp.bfloat16)


def kernel_plan(packed):
    total_rows, width = packed.shape[0], packed.shape[1] // 3
    block_width = 2 * HEAD_DIM if width % (2 * HEAD_DIM) == 0 else width
    groups = width // block_width
    block_rows = min(256, total_rows)
    by_rows = pl.BlockSpec((block_rows, block_width), lambda g, r: (r, g))
    hop = groups if block_width % 128 == 0 else 0
    column = [
        pl.BlockSpec((block_rows, block_width), lambda g, r: (r, g)),
        pl.BlockSpec((total_rows, block_width), lambda g, r: (0, hop + g)),
        pl.BlockSpec((total_rows, block_width), lambda g, r: (0, 2 * hop + g)),
    ]
    heads = block_width // HEAD_DIM
    lse_spec = pl.BlockSpec((1, heads, block_rows), lambda g, r: (g, 0, r))
    lse_shape = jax.ShapeDtypeStruct((groups, heads, total_rows), jnp.float32)
    grid = (groups, total_rows // block_rows)
    params = pltpu.CompilerParams(vmem_limit_bytes=48 * 1024 * 1024)
    return total_rows, width, block_width, by_rows, column, lse_spec, lse_shape, grid, params


def thirds(packed):
    width = packed.shape[1] // 3
    if width % 128 == 0:
        return (packed, packed, packed)
    return tuple(packed[:, part * width : (part + 1) * width] for part in range(3))


def attend(packed):
    total_rows, width, block_width, by_rows, column, lse_spec, lse_shape, grid, params = (
        kernel_plan(packed)
    )
    work = HEAD_DIM * total_rows * total_rows * (width // HEAD_DIM)
    return pl.pallas_call(
        attend_kernel,
        grid=grid,
        in_specs=column,
        out_specs=(by_rows, lse_spec),
        out_shape=(jax.ShapeDtypeStruct((total_rows, width), jnp.float32), lse_shape),
        scratch_shapes=[pltpu.VMEM((block_width, total_rows), jnp.bfloat16)],
        compiler_params=params,
        cost_estimate=pl.CostEstimate(
            flops=8 * work, bytes_accessed=10 * total_rows * width, transcendentals=work // HEAD_DIM
        ),
    )(*thirds(packed))


def attend_back(packed, attended, log_total, grad):
    total_rows, width, block_width, by_rows, column, lse_spec, lse_shape, grid, params = (
        kernel_plan(packed)
    )
    whole = pl.BlockSpec((total_rows, block_width), lambda g, r: (0, g))
    low_shape = jax.ShapeDtypeStruct((total_rows, width), jnp.bfloat16)
    work = HEAD_DIM * total_rows * total_rows * (width // HEAD_DIM)
    return pl.pallas_call(
        attend_back_kernel,
        grid=grid,
        in_specs=column + [by_rows, lse_spec, by_rows],
        out_specs=(by_rows, whole, whole),
        out_shape=(low_shape, low_shape, low_shape),
        scratch_shapes=[
            pltpu.VMEM((block_width, total_rows), jnp.bfloat16),
            pltpu.VMEM((total_rows, block_width), jnp.float32),
            pltpu.VMEM((total_rows, block_width), jnp.float32),
        ],
        compiler_params=params,
        cost_estimate=pl.CostEstimate(
            flops=20 * work, bytes_accessed=20 * total_rows * width, transcendentals=work // HEAD_DIM
        ),
    )(*thirds(packed), attended, log_total, grad)


def group_count(model_width):
    share = model_width // lax.axis_size("ctx")
    return share // 128 if share % 128 == 0 else 1


def to_heads(arrays, group, groups):
    count, me = lax.axis_size("ctx"), lax.axis_index("ctx")
    share = arrays[0].shape[1] // count
    width = share // groups
    received = []
    for step in range(count):
        start = lax.rem(me + step, count) * share + group * width
        piece = jnp.concatenate(
            [lax.dynamic_slice_in_dim(item, start, width, 1) for item in arrays], 1
        )
        if step:
            piece = lax.ppermute(
                piece, "ctx", [(source, (source + step) % count) for source in range(count)]
            )
        received.append(piece)
    return jnp.concatenate(received, 0)


def to_rows(arrays):
    count, me = lax.axis_size("ctx"), lax.axis_index("ctx")
    rows, width = arrays[0].shape[0] // count, arrays[0].shape[1]
    received = []
    for step in range(count):
        piece = jnp.concatenate([item[step * rows : (step + 1) * rows] for item in arrays], 1)
        if step:
            piece = lax.ppermute(
                piece, "ctx", [(source, (source - step) % count) for source in range(count)]
            )
        received.append(piece)
    start = lax.rem(count - me, count) * width
    results = []
    for number in range(len(arrays)):
        turned = [item[:, number * width : (number + 1) * width] for item in received]
        doubled = jnp.concatenate(turned + turned, 1)
        results.append(lax.dynamic_slice_in_dim(doubled, start, count * width, 1))
    return results


def join(groups):
    count = lax.axis_size("ctx")
    if len(groups) == 1:
        return groups[0]
    results = []
    for parts in zip(*groups):
        width = parts[0].shape[1] // count
        pieces = [
            part[:, owner * width : (owner + 1) * width]
            for owner in range(count)
            for part in parts
        ]
        results.append(jnp.concatenate(pieces, 1))
    return results


def local(
    tokens,
    query_key_value_weight,
    attention_output_weight,
    geglu_input_weight,
    geglu_output_weight,
    gain_one,
    gain_two,
    cotangent,
):
    local_rows = tokens.shape[1]
    model_width = tokens.shape[2]
    hidden_width = geglu_output_weight.shape[0]
    score_scale = HEAD_DIM ** (-0.5)
    full_qkv, full_attn, full_in, full_out, full_one, full_two = (
        lax.all_gather(query_key_value_weight, "fsdp", axis=0, tiled=True),
        lax.all_gather(attention_output_weight, "fsdp", axis=0, tiled=True),
        lax.all_gather(geglu_input_weight, "fsdp", axis=0, tiled=True),
        lax.all_gather(geglu_output_weight, "fsdp", axis=1, tiled=True),
        *lax.all_gather(jnp.stack([gain_one, gain_two]), "fsdp", axis=1, tiled=True),
    )
    inputs = tokens[0].astype(jnp.float32)
    normed_one, inv_one = normalize(inputs)
    hidden_after_attention = (normed_one * full_one.astype(jnp.float32)).astype(jnp.bfloat16)
    query_key_value = jnp.dot(hidden_after_attention, full_qkv, preferred_element_type=jnp.float32)
    cosine, sine = rope_tables(lax.axis_index("ctx") * local_rows, local_rows)
    head_shape = (local_rows, HEADS, HEAD_DIM)
    query = rotate(query_key_value[:, :model_width].reshape(head_shape), cosine, sine)
    query = (query.astype(jnp.bfloat16) * score_scale).reshape(local_rows, model_width)
    keys = rotate(
        query_key_value[:, model_width : 2 * model_width].reshape(head_shape), cosine, sine
    ).astype(jnp.bfloat16)
    keys = keys.reshape(local_rows, model_width)
    values = query_key_value[:, 2 * model_width :].astype(jnp.bfloat16)
    groups = group_count(model_width)
    packed = [to_heads((query, keys, values), group, groups) for group in range(groups)]
    forward = [attend(item) for item in packed]
    (attn_low,) = join([to_rows((item[0].astype(jnp.bfloat16),)) for item in forward])
    middle_activation = inputs + jnp.dot(attn_low, full_attn, preferred_element_type=jnp.float32)
    normed_two, inv_two = normalize(middle_activation)
    hidden_after_feedforward = (normed_two * full_two.astype(jnp.float32)).astype(jnp.bfloat16)
    projected_up_rows = jnp.dot(
        hidden_after_feedforward, full_in, preferred_element_type=jnp.float32
    )
    gate_in = projected_up_rows[:, :hidden_width]
    gate_up = projected_up_rows[:, hidden_width:]
    normal_cdf = 0.5 * (1.0 + lax.erf(gate_in * (1.0 / math.sqrt(2.0))))
    normal_pdf = jnp.exp(-0.5 * gate_in * gate_in) * (1.0 / math.sqrt(2.0 * math.pi))
    activated = gate_in * normal_cdf
    hidden_state = (activated * gate_up).astype(jnp.bfloat16)
    mixed = (
        middle_activation + jnp.dot(hidden_state, full_out, preferred_element_type=jnp.float32)
    ).astype(jnp.bfloat16)
    back_qkv, back_attn, back_in, back_out, back_one, back_two = (
        full_qkv,
        full_attn,
        full_in,
        full_out,
        full_one,
        full_two,
    )
    grad_mixed = cotangent[0]
    grad_wout = jnp.einsum(
        "rf,rd->fd", hidden_state, grad_mixed, preferred_element_type=jnp.float32
    )
    grad_hidden = jnp.einsum("rd,fd->rf", grad_mixed, back_out, preferred_element_type=jnp.float32)
    grad_up = jnp.concatenate(
        [grad_hidden * gate_up * (normal_cdf + gate_in * normal_pdf), grad_hidden * activated], -1
    ).astype(jnp.bfloat16)
    grad_win = jnp.einsum(
        "rd,rf->df", hidden_after_feedforward, grad_up, preferred_element_type=jnp.float32
    )
    grad_htwo = jnp.einsum("rf,df->rd", grad_up, back_in, preferred_element_type=jnp.float32)
    grad_two = jnp.sum(grad_htwo * normed_two, 0)
    grad_middle = grad_mixed.astype(jnp.float32) + norm_back(
        grad_htwo * back_two.astype(jnp.float32), normed_two, inv_two
    )
    part_win = lax.psum_scatter(
        grad_win.astype(jnp.bfloat16), "fsdp", scatter_dimension=0, tiled=True
    )
    part_wout = lax.psum_scatter(
        grad_wout.astype(jnp.bfloat16), "fsdp", scatter_dimension=1, tiled=True
    )
    grad_branch = grad_middle.astype(jnp.bfloat16)
    grad_wattn = jnp.einsum("rd,re->de", attn_low, grad_branch, preferred_element_type=jnp.float32)
    part_wattn = lax.psum_scatter(
        grad_wattn.astype(jnp.bfloat16), "fsdp", scatter_dimension=0, tiled=True
    )
    sum_win, sum_wout, sum_wattn = lax.psum((part_win, part_wout, part_wattn), "ctx")
    grad_attn = jnp.einsum("re,de->rd", grad_branch, back_attn, preferred_element_type=jnp.float32)
    grad_attn = grad_attn.astype(jnp.bfloat16)
    back_query, back_keys, grad_v = join(
        [
            to_rows(
                attend_back(packed[group], *forward[group], to_heads((grad_attn,), group, groups))
            )
            for group in range(groups)
        ]
    )
    grad_q = rotate(back_query.reshape(head_shape).astype(jnp.float32), cosine, -sine)
    grad_k = rotate(back_keys.reshape(head_shape).astype(jnp.float32), cosine, -sine)
    grad_qkv_rows = jnp.concatenate(
        [
            grad_q.reshape(local_rows, model_width).astype(jnp.bfloat16),
            grad_k.reshape(local_rows, model_width).astype(jnp.bfloat16),
            grad_v,
        ],
        -1,
    )
    grad_wqkv = jnp.einsum(
        "rd,re->de", hidden_after_attention, grad_qkv_rows, preferred_element_type=jnp.float32
    )
    grad_hone = jnp.einsum("re,de->rd", grad_qkv_rows, back_qkv, preferred_element_type=jnp.float32)
    grad_one = jnp.sum(grad_hone * normed_one, 0)
    grad_inputs = grad_middle + norm_back(
        grad_hone * back_one.astype(jnp.float32), normed_one, inv_one
    )
    sum_win, sum_wout, sum_wattn, grad_wqkv = lax.optimization_barrier(
        (sum_win, sum_wout, sum_wattn, grad_wqkv.astype(jnp.bfloat16))
    )
    part_wqkv = lax.psum_scatter(grad_wqkv, "fsdp", scatter_dimension=0, tiled=True)
    sum_wqkv = lax.psum(part_wqkv, "ctx")
    sum_win, sum_wout, sum_wqkv, sum_wattn = (
        item.astype(jnp.float32) for item in (sum_win, sum_wout, sum_wqkv, sum_wattn)
    )
    gains = lax.psum(jnp.stack([grad_one, grad_two]), ("fsdp", "ctx"))
    shard = gain_one.shape[0]
    gains = lax.dynamic_slice_in_dim(gains, lax.axis_index("fsdp") * shard, shard, 1)
    sum_one, sum_two = gains[0], gains[1]
    return (
        mixed[None],
        grad_inputs[None],
        sum_wqkv,
        sum_wattn,
        sum_win,
        sum_wout,
        sum_one,
        sum_two,
    )


def solution(mesh):
    placed = (
        P("fsdp", "ctx", None),
        P("fsdp", None),
        P("fsdp", None),
        P("fsdp", None),
        P(None, "fsdp"),
        P("fsdp"),
        P("fsdp"),
        P("fsdp", "ctx", None),
    )
    return jax.shard_map(
        local,
        mesh=mesh,
        in_specs=placed,
        out_specs=(
            P("fsdp", "ctx", None),
            P("fsdp", "ctx", None),
            P("fsdp", None),
            P("fsdp", None),
            P("fsdp", None),
            P(None, "fsdp"),
            P("fsdp"),
            P("fsdp"),
        ),
        check_vma=False,
    )
```
